128 devices in a mesh: seq: 32 (over y, x_hi, z), head: 4 (over x_lo, core).
Axes of the slice: x: 4 (x_hi: 2, x_lo: 2; x = x_hi * 2 + x_lo), y: 4, z: 4, core: 2. Of those that a mesh axis runs over, the one named last changes fastest.
Arguments:
- mixer_input: bfloat16 [65536, 5120], P('seq', 'head'), may hold values from -6 to 6
- write_map: bfloat16 [65536, 128], P('seq', 'head'), may hold values from -0.5 to 0.5
- read_map: bfloat16 [65536, 128], P('seq', 'head'), may hold values from -6 to 6
- step_size: float32 [80, 65536], P('head', 'seq'), may hold values from 0 to 0.5
- log_decay: float32 [80, 65536], P('head', 'seq'), may hold values from -3 to 0
- skip_gain: float32 [80], P('head'), may hold values from 0.5 to 1.5
- level_table: float32 [9, 8], replicated, may hold values from 0.5 to 2
- level_index: int32 [9, 65536], P(None, 'seq'), may hold values from 0 to 7
Outputs:
- mixer_output: bfloat16 [65536, 5120], P('seq', 'head')
The draws below stay inside these ranges and needn't reach their ends.
All inputs are finite; a program needn't handle non-finite values.
Results may differ from the reference program's by a relative error of at most 0.0043.
Values may be sent and summed in bfloat16 or wider, within the bound.
A program may use at most 256 MiB of HBM per device.

```python
import math
import jax
import jax.numpy as jnp
from jax import lax

HEAD_TOTAL = 80
HEAD_DIM = 64
STATE = 128
BLOCK = 256
LEVEL_CHOICES = 8
SEQUENCE_TOKENS = 65536
LEVELS = 9


def decay_rates(key):
    base_key = jax.random.fold_in(key, 7)
    ranking = jax.random.permutation(jax.random.fold_in(base_key, 1), HEAD_TOTAL)
    fast_count = max(1, HEAD_TOTAL // 8)
    lasting_count = HEAD_TOTAL // 2
    middle_count = (HEAD_TOTAL - lasting_count - fast_count) // 2
    fast_rate = 1.0 / jax.random.uniform(jax.random.fold_in(base_key, 2), (HEAD_TOTAL,), minval=30.0, maxval=50.0)
    slow_rate = jax.random.uniform(jax.random.fold_in(base_key, 3), (HEAD_TOTAL,), minval=0.1, maxval=0.6) / SEQUENCE_TOKENS
    medium_rate = jax.random.uniform(jax.random.fold_in(base_key, 4), (HEAD_TOTAL,), minval=0.64, maxval=1.0) / BLOCK
    gentle_rate = jax.random.uniform(jax.random.fold_in(base_key, 5), (HEAD_TOTAL,), minval=0.16, maxval=0.19) / BLOCK
    return jnp.where(ranking < fast_count, fast_rate, jnp.where(ranking < fast_count + middle_count, medium_rate, jnp.where(ranking < HEAD_TOTAL - lasting_count, gentle_rate, slow_rate)))


def rough_factor(key, salt):
    return jnp.exp(jax.random.uniform(jax.random.fold_in(key, salt), (HEAD_TOTAL, SEQUENCE_TOKENS), minval=-0.7, maxval=0.7))


def draw_log_decay(key, part):
    forget_rate = decay_rates(key)
    block_total = SEQUENCE_TOKENS // BLOCK
    block_multiplier = jnp.exp(jax.random.uniform(jax.random.fold_in(key, 21), (HEAD_TOTAL, block_total), minval=-0.7, maxval=0.7))
    block_multiplier = jnp.repeat(block_multiplier, BLOCK, axis=1)
    token_multiplier = rough_factor(key, 22)
    spike_positions = jax.random.randint(jax.random.fold_in(key, 23), (2,), 0, SEQUENCE_TOKENS)
    spike_lengths = jnp.log(jax.random.uniform(jax.random.fold_in(key, 24), (2, HEAD_TOTAL), minval=0.5, maxval=0.8))
    struck_flags = jnp.arange(SEQUENCE_TOKENS)[None, :] == spike_positions[:, None]
    spike_events = jnp.sum(jnp.where(struck_flags[:, None, :], spike_lengths[:, :, None], 0.0), axis=0)
    return (-forget_rate[:, None] * block_multiplier * token_multiplier + spike_events).astype(jnp.float32)


def draw_step_size(key, part):
    forget_rate = decay_rates(key)
    memory = jnp.minimum(1.0 / forget_rate, SEQUENCE_TOKENS * 1.0)
    return (rough_factor(key, 31) / jnp.sqrt(memory)[:, None]).astype(jnp.float32)


def set_ends(values, stream_key, low, top_value):
    longest = values.shape.index(max(values.shape))
    spots = []
    for shift in (0, 1):
        where = [jax.random.randint(jax.random.fold_in(stream_key, axis), (), 0, length) for axis, length in enumerate(values.shape)]
        where[longest] = (where[longest] + shift) % values.shape[longest]
        spots.append(tuple(where))
    return values.at[spots[0]].set(low).at[spots[1]].set(top_value)


def levels(rng, dims, pieces, smallest, largest):
    loudness = 1.0
    for dim, shards_of in pieces:
        heights = jax.random.uniform(jax.random.fold_in(jax.random.fold_in(rng, 6), dim), (shards_of,), jnp.float32, smallest / len(pieces), largest / len(pieces))
        loudness = loudness * jnp.repeat(jnp.exp(heights), dims[dim] // shards_of).reshape((-1,) + (1,) * (len(dims) - 1 - dim))
    return loudness


def normal_values(own_key, dims, spread, limit, cuts=(), kind=jnp.bfloat16):
    entries = spread * jax.random.normal(own_key, dims, jnp.float32)
    if cuts:
        entries = entries * levels(own_key, dims, cuts, -0.22, 0.18)
    return jnp.clip(entries, -limit, limit).astype(kind)


def setup_inputs(seed: int = 0) -> dict:
    seeds = jax.random.split(jax.random.key(seed), 9)
    return {
        "mixer_input": normal_values(seeds[0], (SEQUENCE_TOKENS, HEAD_TOTAL * HEAD_DIM), 1.0, 6.0, ((0, 32), (1, 4))),
        "write_map": normal_values(seeds[1], (SEQUENCE_TOKENS, STATE), STATE ** -0.5, 0.5, ((0, 32), (1, 4))),
        "read_map": normal_values(seeds[2], (SEQUENCE_TOKENS, STATE), 1.0, 6.0, ((0, 32), (1, 4))),
        "step_size": draw_step_size(jax.random.fold_in(seeds[8], 71), 0),
        "log_decay": draw_log_decay(jax.random.fold_in(seeds[8], 71), 0),
        "skip_gain": jnp.clip(0.5 + 1.0 * jax.random.uniform(seeds[5], (HEAD_TOTAL,), jnp.float32) ** levels(seeds[5], (HEAD_TOTAL,), ((0, 4),), -0.2, 0.2), 0.5, 1.5),
        "level_table": jnp.clip(jnp.exp(jax.random.uniform(seeds[6], (LEVELS, LEVEL_CHOICES), jnp.float32, math.log(0.5), math.log(2.0))), 0.5, 2.0),
        "level_index": set_ends(jax.random.randint(seeds[7], (LEVELS, SEQUENCE_TOKENS), 0, LEVEL_CHOICES), jax.random.fold_in(seeds[7], 1), 0, LEVEL_CHOICES - 1).astype(jnp.int32),
    }


def tree_merge(lower_state, lower_total, upper_state, upper_total):
    merged = jnp.exp(upper_total)[..., None, None] * lower_state + upper_state
    return merged, lower_total + upper_total


def reference(mixer_input, write_map, read_map, step_size, log_decay, skip_gain, level_table, level_index):
    block_count = SEQUENCE_TOKENS // BLOCK
    tree_depth = LEVELS - 1
    level_weight = jnp.take_along_axis(level_table, level_index, axis=1)
    write_rows = write_map.astype(jnp.float32).reshape(block_count, BLOCK, STATE)
    read_rows = read_map.astype(jnp.float32).reshape(block_count, BLOCK, STATE)
    scores = jnp.einsum("btn,bsn->bts", read_rows, write_rows)
    queries = (level_weight[1:].T.reshape(block_count, BLOCK, tree_depth, 1) * read_rows[:, :, None, :]).reshape(block_count, BLOCK, tree_depth * STATE)
    causal = jnp.tril(jnp.ones((BLOCK, BLOCK), dtype=bool))
    positions = jnp.arange(block_count, dtype=jnp.int32)
    first_weight = level_weight[0].reshape(block_count, BLOCK, 1)

    def head_out(packed):
        head_input, head_step, head_decay, head_skip = packed
        decay_sum = jnp.cumsum(head_decay.reshape(block_count, BLOCK), axis=1)
        block_decay = decay_sum[:, -1]
        input_f32 = head_input.astype(jnp.float32).reshape(block_count, BLOCK, HEAD_DIM)
        step_block = head_step.reshape(block_count, BLOCK)
        inputs = (input_f32 * step_block[:, :, None]).astype(jnp.bfloat16)
        gap = jnp.where(causal[None], decay_sum[:, :, None] - decay_sum[:, None, :], -jnp.inf)
        mixing = (scores * jnp.exp(gap)).astype(jnp.bfloat16)
        intra_part = jnp.einsum("bts,bsp->btp", mixing.astype(jnp.float32), inputs.astype(jnp.float32))
        end_inputs = (input_f32 * (step_block * jnp.exp(block_decay[:, None] - decay_sum))[:, :, None]).astype(jnp.bfloat16)
        level_state = jnp.einsum("bsn,bsp->bnp", write_rows, end_inputs.astype(jnp.float32))
        level_total = block_decay
        running = jnp.zeros((block_count,), jnp.float32)
        states = []
        for bit_pos in range(tree_depth):
            shifted = positions >> bit_pos
            bit_flag = (shifted & 1).astype(jnp.float32)
            bucket_at = jnp.maximum(shifted - 1, 0)
            states.append((bit_flag * jnp.exp(running))[:, None, None] * level_state[bucket_at])
            running = running + bit_flag * level_total[bucket_at]
            if bit_pos + 1 < tree_depth:
                paired_state = level_state.reshape(-1, 2, STATE, HEAD_DIM)
                paired_total = level_total.reshape(-1, 2)
                level_state, level_total = tree_merge(paired_state[:, 0], paired_total[:, 0], paired_state[:, 1], paired_total[:, 1])
        stacked = jnp.stack(states, axis=1).reshape(block_count, tree_depth * STATE, HEAD_DIM)
        inter_part = jnp.einsum("btk,bkp->btp", queries, stacked, precision=lax.Precision.HIGHEST)
        result = first_weight * intra_part + jnp.exp(decay_sum)[:, :, None] * inter_part + head_skip * input_f32
        return result.astype(jnp.bfloat16).reshape(SEQUENCE_TOKENS, HEAD_DIM)

    head_inputs = mixer_input.reshape(SEQUENCE_TOKENS, HEAD_TOTAL, HEAD_DIM).transpose(1, 0, 2)
    outputs = lax.map(head_out, (head_inputs, step_size, log_decay, skip_gain))
    return outputs.transpose(1, 0, 2).reshape(SEQUENCE_TOKENS, HEAD_TOTAL * HEAD_DIM)
```

```python
import math

import jax
import jax.numpy as jnp
import numpy as np
from jax import lax
from jax.experimental import pallas as pl
from jax.experimental.pallas import tpu as pltpu
from jax.sharding import PartitionSpec as P

SUB = 128
NSUB = 16
TOKENS = SUB * NSUB
HEADS = 20
WIDE = 256
CHUNKS = 5
STATE = 128
SHARE = 32
LEVELS = 9
TABLE = 8
LOG2E = math.log2(math.e)
MESH = pl.DeviceIdType.MESH
BF = jnp.bfloat16
F32 = jnp.float32

COL_MIX, COL_END, COL_OUT, COL_FAR, COL_LEVEL, COL_SUM = 0, 24, 48, 72, 96, 104
LEVEL_LANE = [COL_LEVEL + i for i in range(8)] + [20]
SPREAD_BASE = (COL_END, COL_OUT, COL_FAR, COL_SUM)


def range_rows():
    rows = {}

    def row(lo, hi):
        return rows.setdefault((lo, hi), len(rows))

    merge = {}
    for i in range(4):
        for k in range(NSUB >> (i + 1)):
            merge[i, k] = row((2 * k + 1) << i, (2 * k + 2) << i)
    scale = {}
    for j in range(NSUB):
        bits = [i for i in range(4) if j >> i & 1]
        for i in bits[1:]:
            scale[j, i] = row((j >> i) << i, j)
    total = row(0, NSUB)
    return rows, merge, scale, total


ROWS, MERGE, SCALE, TOTAL = range_rows()
SKIP_ROW = 63
LOCAL = [(j, i) for j in range(NSUB) for i in range(4) if j >> i & 1]
LOCAL_AT = {pair: n for n, pair in enumerate(LOCAL)}


def range_matrix():
    w = np.zeros((64, 128), np.float32)
    for (lo, hi), r in ROWS.items():
        for part in range(3):
            w[r, part * NSUB + lo : part * NSUB + hi] = 1.0
    return w


def dot(a, b):
    return jnp.dot(a, b, preferred_element_type=F32)


def split2(v):
    hi = v.astype(BF)
    return hi, (v - hi.astype(F32)).astype(BF)


def split3(v):
    hi = v.astype(BF)
    rest = v - hi.astype(F32)
    mid = rest.astype(BF)
    return hi, mid, (rest - mid.astype(F32)).astype(BF)


def kernel(
    x_hbm, b_own, c_own, step_in, decay_in, skip_in, table_in, index_in, ranges_in,
    out_hbm,
    x_s, b_t, c_t, ld_s, st_s, lw_s, tab_s, m_s, rv_s, colf, colhl, tots, tots3,
    rexp, spread, tree, loc, scm, qs, part, out_s, zbuf, xbuf, ybuf, rbuf,
    tz, tx, ty, secc, secw,
    bs, br, cs, cr, tzs, tzr, txs, txr, tys, tyr, zs, zr, xs, xr, ys, yr, ins, outs,
):
    seq = lax.axis_index("seq")
    me = lax.axis_index("head")
    z, xh, y = seq % 4, (seq // 4) % 2, seq // 8
    sib = me // 2 * 2 + (me + 1) % 2
    opp = (me + 2) % 4

    def at(z=z, xh=xh, y=y, h=me):
        return {"seq": (y * 2 + xh) * 4 + z, "head": h}

    def remote(src, dst, ssem, rsem, where):
        return pltpu.make_async_remote_copy(
            src_ref=src, dst_ref=dst, send_sem=ssem, recv_sem=rsem,
            device_id=where, device_id_type=MESH,
        )

    def cols(j):
        return pl.ds(pl.multiple_of(j * SUB, SUB), SUB)

    peers = [at(h=sib), at(h=opp)]
    peers += [at(z=(z + d) % 4) for d in (1, 2, 3)]
    peers += [at(xh=1 - xh)]
    peers += [at(y=(y + d) % 4) for d in (1, 2, 3)]
    barrier = pltpu.get_barrier_semaphore()
    for p in peers:
        pl.semaphore_signal(barrier, inc=1, device_id=p, device_id_type=MESH)

    def x_in(c):
        return pltpu.make_async_copy(
            x_hbm.at[:, pl.ds(pl.multiple_of(c * WIDE, WIDE), WIDE)], x_s.at[c], ins.at[c]
        )

    for c in range(CHUNKS):
        x_in(c).start()

    own_rows = pl.ds(pl.multiple_of(me * SHARE, SHARE), SHARE)
    opp_rows = pl.ds(pl.multiple_of(opp * SHARE, SHARE), SHARE)
    b_t[own_rows, :] = b_own[...]
    c_t[own_rows, :] = c_own[...]

    def share_copies(buf, ss, rs):
        own = buf.at[own_rows]
        far = buf.at[opp_rows]
        return (
            remote(own, own, ss.at[0], rs.at[0], at(h=opp)),
            remote(own, own, ss.at[1], rs.at[1], at(h=sib)),
            remote(far, far, ss.at[2], rs.at[2], at(h=sib)),
        )

    b_copies = share_copies(b_t, bs, br)
    c_copies = share_copies(c_t, cs, cr)
    pl.semaphore_wait(barrier, len(peers))
    for k in (0, 1):
        b_copies[k].start()
    for k in (0, 1):
        c_copies[k].start()

    ld_s[...] = jnp.zeros_like(ld_s)
    st_s[...] = jnp.zeros_like(st_s)
    ld_s[0:HEADS, :] = decay_in[...]
    st_s[0:HEADS, :] = step_in[...]
    tab_s[...] = jnp.zeros_like(tab_s)
    tab_s[:, 0:LEVELS] = table_in[...]
    tab_t = tab_s[...].T
    lw_s[...] = jnp.ones_like(lw_s)
    weight = jnp.zeros((LEVELS, TOKENS), F32)
    index = index_in[...]
    for e in range(TABLE):
        weight = weight + jnp.where(index == e, tab_t[0:LEVELS, e : e + 1], 0.0)
    lw_s[0:LEVELS, :] = weight

    lanes3 = lax.broadcasted_iota(jnp.int32, (3 * SUB, SUB), 1)
    rows3 = lax.broadcasted_iota(jnp.int32, (3 * SUB, SUB), 0) & (SUB - 1)
    upper = jnp.where(rows3 <= lanes3, 1.0, 0.0).astype(BF)

    def prepare(j, off):
        here = cols(j)
        hi, mid, lo = split3(ld_s[:, here])
        d = dot(jnp.concatenate([hi, mid, lo], axis=1), upper)[0:24]
        total = jnp.broadcast_to(d[:, SUB - 1 : SUB], (24, SUB))
        log_step = jnp.log(st_s[0:24, here]) * LOG2E
        lw = lw_s[:, here]
        d2 = d * LOG2E
        rv = d2 - log_step
        for c in range(CHUNKS):
            rv_s[c, 0:4, here] = rv[4 * c : 4 * c + 4]
        m_s[0:24, :] = d2 + jnp.log(lw[0:1]) * LOG2E
        m_s[20:21, :] = lw[8:9]
        m_s[COL_END : COL_END + 24, :] = jnp.exp2((total - d) * LOG2E + log_step)
        m_s[COL_OUT : COL_OUT + 24, :] = jnp.exp2(d2)
        m_s[COL_FAR : COL_FAR + 24, :] = jnp.exp2((d + off) * LOG2E)
        m_s[COL_LEVEL : COL_LEVEL + 8, :] = lw[0:8]
        m_s[COL_SUM : COL_SUM + 24, :] = d
        mt = m_s[...].T
        colf[here, :] = mt
        hi2, lo2 = split2(mt)
        colhl[here, 0:SUB] = hi2
        colhl[here, SUB : 2 * SUB] = lo2
        tots[pl.ds(j, 1), :] = mt[SUB - 1 : SUB, :]
        return off + total

    lax.fori_loop(0, NSUB, prepare, jnp.zeros((24, SUB), F32))

    k_at = lax.broadcasted_iota(jnp.int32, (2 * SUB, WIDE), 0) & (SUB - 1)
    head_at = k_at - (lax.broadcasted_iota(jnp.int32, (2 * SUB, WIDE), 1) >> 6)

    def build(c, carry):
        for g, base in enumerate(SPREAD_BASE):
            spread[g, c] = jnp.where(head_at == base + 4 * c, 1.0, 0.0).astype(BF)
        return carry

    lax.fori_loop(0, CHUNKS, build, 0)

    tots3[...] = jnp.zeros_like(tots3)
    for n, piece in enumerate(split3(tots[...])):
        tots3[n * NSUB : (n + 1) * NSUB, :] = piece
    range_log = dot(ranges_in[...], tots3[...])
    lane_at = lax.broadcasted_iota(jnp.int32, (64, SUB), 1)
    range_log = jnp.where(lane_at >= COL_SUM, range_log, 0.0)
    own_total = jnp.broadcast_to(range_log[TOTAL : TOTAL + 1], (8, SUB))
    tz[z] = own_total

    def tz_copy(d):
        return remote(tz.at[z], tz.at[z], tzs.at[d - 1], tzr.at[d - 1], at(z=(z + d) % 4))

    def tz_arrival(d):
        k = (z - d) % 4
        return remote(tz.at[k], tz.at[k], tzs.at[d - 1], tzr.at[d - 1], at(z=k))

    for d in (1, 2, 3):
        tz_copy(d).start()

    tab_s[...] = jnp.zeros_like(tab_s)
    tab_s[0:1, 0:HEADS] = skip_in[...]
    skip_row = pltpu.roll(tab_s[...], COL_SUM, 1)[0:1]
    row_at = lax.broadcasted_iota(jnp.int32, (64, SUB), 0)
    factor = jnp.where(row_at == SKIP_ROW, skip_row, jnp.exp(range_log))
    factor = jnp.concatenate(split2(factor), axis=1)

    def spread_rows(c, carry):
        rexp[c] = dot(factor, spread[3, c])
        return carry

    lax.fori_loop(0, CHUNKS, spread_rows, 0)

    b_copies[0].wait_recv()
    b_copies[2].start()
    c_copies[0].wait_recv()
    c_copies[2].start()
    b_copies[1].wait_recv()
    b_copies[2].wait_recv()

    for d in (1, 2, 3):
        tz_arrival(d).wait_recv()
    far_t = [tz[k, 0:1] for k in range(4)]
    tx[xh] = jnp.broadcast_to(far_t[0] + far_t[1] + far_t[2] + far_t[3], (8, SUB))
    tx_copy = remote(tx.at[xh], tx.at[xh], txs, txr, at(xh=1 - xh))
    tx_copy.start()

    def z_copy(c, d):
        return remote(
            zbuf.at[c, z], zbuf.at[c, z], zs.at[c, d - 1], zr.at[c, d - 1], at(z=(z + d) % 4)
        )

    def z_arrival(c, d):
        k = (z - d) % 4
        return remote(zbuf.at[c, k], zbuf.at[c, k], zs.at[c, d - 1], zr.at[c, d - 1], at(z=k))

    first = {0: 0, 1: 16, 2: 24, 3: 28}

    def states(c, carry):
        x_in(c).wait()

        def one(j, carry):
            here = cols(j)
            end = dot(colhl[here, :], spread[0, c])
            scaled = (x_s[c, here, :].astype(F32) * end).astype(BF)
            tree[j] = dot(b_t[:, here], scaled)
            return carry

        lax.fori_loop(0, NSUB, one, 0)
        for i in range(4):
            for k in range(NSUB >> (i + 1)):
                r = MERGE[i, k]
                merged = (
                    rexp[c, r : r + 1, :] * tree[first[i] + 2 * k] + tree[first[i] + 2 * k + 1]
                )
                if i < 3:
                    tree[first[i + 1] + k] = merged
                else:
                    zbuf[c, z] = merged.astype(BF)
        for d in (1, 2, 3):
            z_copy(c, d).start()
        for (j, i), n in LOCAL_AT.items():
            value = tree[first[i] + (j >> i) - 1]
            if (j, i) in SCALE:
                r = SCALE[j, i]
                value = rexp[c, r : r + 1, :] * value
            loc[c, n * STATE : (n + 1) * STATE, :] = value.astype(BF)
        return carry

    lax.fori_loop(0, CHUNKS, states, 0)

    tx_copy.wait_recv()
    ty[y] = jnp.broadcast_to(tx[0, 0:1] + tx[1, 0:1], (8, SUB))

    def ty_copy(d):
        return remote(ty.at[y], ty.at[y], tys.at[d - 1], tyr.at[d - 1], at(y=(y + d) % 4))

    def ty_arrival(d):
        k = (y - d) % 4
        return remote(ty.at[k], ty.at[k], tys.at[d - 1], tyr.at[d - 1], at(y=k))

    for d in (1, 2, 3):
        ty_copy(d).start()

    c_copies[1].wait_recv()
    c_copies[2].wait_recv()
    causal = lax.broadcasted_iota(jnp.int32, (SUB, SUB), 0) >= lax.broadcasted_iota(
        jnp.int32, (SUB, SUB), 1
    )

    def queries(j, carry):
        here = cols(j)
        c_rows = c_t[:, here].astype(F32).T
        scm[j] = jnp.where(causal, dot(c_rows.astype(BF), b_t[:, here]), 0.0)
        tile = colf[here, :]
        for i, lane in enumerate(LEVEL_LANE):
            qs[here, i * STATE : (i + 1) * STATE] = (tile[:, lane : lane + 1] * c_rows).astype(BF)
        return carry

    lax.fori_loop(0, NSUB, queries, 0)

    for d in (1, 2, 3):
        ty_arrival(d).wait_recv()

    t0, t1, t2, t3 = far_t
    u0, u1 = tx[0, 0:1], tx[1, 0:1]
    v1, v2 = ty[1, 0:1], ty[2, 0:1]

    def only(flag, row):
        return jnp.where(flag, row, 0.0)

    run2 = only(z > 0, t0) + only(z > 1, t1) + only(z > 2, t2)
    run3 = run2 + only(xh == 1, u0)
    run4 = run3 + only(y == 3, v2)
    low_run = only(z == 3, t2)
    upper_z, upper_y = z >= 2, y >= 2
    weights = [
        jnp.exp(t1 + t2 + t3),
        jnp.exp(t2 + t3),
        jnp.exp(t3),
        only(upper_z, jnp.exp(t1 + low_run)),
        only(upper_z, jnp.exp(low_run)),
        only(xh == 1, jnp.exp(run2)),
        jnp.exp(u1),
        jnp.exp(run3),
        jnp.exp(v1 + run4),
        jnp.exp(run4),
    ]
    secc[...] = jnp.zeros_like(secc)
    for n, w in enumerate(weights):
        secc[n : n + 1, :] = w
    compact = jnp.concatenate(split2(secc[...]), axis=1)

    def spread_weights(c, carry):
        secw[c] = dot(compact, spread[3, c])
        return carry

    lax.fori_loop(0, CHUNKS, spread_weights, 0)

    def x_copy(c):
        return remote(xbuf.at[c, xh], xbuf.at[c, xh], xs.at[c], xr.at[c], at(xh=1 - xh))

    def x_arrival(c):
        k = 1 - xh
        return remote(xbuf.at[c, k], xbuf.at[c, k], xs.at[c], xr.at[c], at(xh=k))

    def y_copy(c, d):
        return remote(
            ybuf.at[c, y], ybuf.at[c, y], ys.at[c, d - 1], yr.at[c, d - 1], at(y=(y + d) % 4)
        )

    def y_arrival(c, d):
        k = (y - d) % 4
        return remote(ybuf.at[c, k], ybuf.at[c, k], ys.at[c, d - 1], yr.at[c, d - 1], at(y=k))

    def after_z(c):
        for d in (1, 2, 3):
            z_arrival(c, d).wait_recv()
        w = [secw[c, n : n + 1, :] for n in range(5)]
        s = [zbuf[c, k].astype(F32) for k in range(4)]
        xbuf[c, xh] = (w[0] * s[0] + w[1] * s[1] + (w[2] * s[2] + s[3])).astype(BF)
        x_copy(c).start()
        rbuf[c, 0:STATE, :] = jnp.where(
            z % 2 == 1, zbuf[c, jnp.maximum(z - 1, 0)].astype(F32), 0.0
        ).astype(BF)
        rbuf[c, STATE : 2 * STATE, :] = (w[3] * s[0] + w[4] * s[1]).astype(BF)

    def after_x(c):
        x_arrival(c).wait_recv()
        s = [xbuf[c, k].astype(F32) for k in range(2)]
        ybuf[c, y] = (secw[c, 6:7, :] * s[0] + s[1]).astype(BF)
        for d in (1, 2, 3):

            @pl.when(y + d < 4)
            def _():
                y_copy(c, d).start()

        rbuf[c, 2 * STATE : 3 * STATE, :] = (secw[c, 5:6, :] * s[0]).astype(BF)

    def after_y(c):
        for d in (1, 2, 3):

            @pl.when(y >= d)
            def _():
                y_arrival(c, d).wait_recv()

        near = secw[c, 7:8, :] * ybuf[c, jnp.maximum(y - 1, 0)].astype(F32)
        rbuf[c, 3 * STATE : 4 * STATE, :] = jnp.where(y % 2 == 1, near, 0.0).astype(BF)
        wide = secw[c, 8:9, :] * ybuf[c, 0].astype(F32) + secw[c, 9:10, :] * ybuf[c, 1].astype(F32)
        rbuf[c, 4 * STATE : 5 * STATE, :] = jnp.where(upper_y, wide, 0.0).astype(BF)

    low_half = lax.broadcasted_iota(jnp.int32, (SUB, SUB), 1) < 64

    def local_part(c):
        turn = lax.rem(SUB - 4 * c, SUB)
        skip = rexp[c, SKIP_ROW : SKIP_ROW + 1, :]
        for j in range(NSUB):
            here = pl.ds(j * SUB, SUB)
            tile = pltpu.roll(colf[here, :], turn, 1)
            masked = scm[j]
            xt = x_s[c, here, :]
            xf = xt.astype(F32)
            halves = []
            for pair in range(2):
                mixes = []
                for k in (2 * pair, 2 * pair + 1):
                    gap = tile[:, k : k + 1] - rv_s[c, k : k + 1, here]
                    mixes.append((masked * jnp.exp2(jnp.minimum(gap, 64.0))).astype(BF))
                xp = xf[:, pair * SUB : (pair + 1) * SUB]
                both = jnp.concatenate(
                    [
                        jnp.where(low_half, xp, 0.0).astype(BF),
                        jnp.where(low_half, 0.0, xp).astype(BF),
                    ],
                    axis=0,
                )
                halves.append(dot(jnp.concatenate(mixes, axis=1), both))
            result = jnp.concatenate(halves, axis=1) + skip * xf
            bits = [i for i in range(4) if j >> i & 1]
            if bits:
                q = jnp.concatenate([qs[here, i * STATE : (i + 1) * STATE] for i in bits], axis=1)
                lo = LOCAL_AT[j, bits[0]] * STATE
                near = dot(q, loc[c, lo : lo + len(bits) * STATE, :])
                result = result + dot(colhl[here, :], spread[1, c]) * near
            part[c, here, :] = result

    def out_copy(c):
        return pltpu.make_async_copy(
            out_s.at[c], out_hbm.at[:, pl.ds(pl.multiple_of(c * WIDE, WIDE), WIDE)], outs.at[c]
        )

    def finish(c):
        def one(j, carry):
            here = pl.ds(pl.multiple_of(j * 256, 256), 256)
            far = dot(qs[here, 4 * STATE : 9 * STATE], rbuf[c])
            result = part[c, here, :] + dot(colhl[here, :], spread[2, c]) * far
            out_s[c, here, :] = result.astype(BF)
            return carry

        lax.fori_loop(0, TOKENS // 256, one, 0)
        out_copy(c).start()

    def step(i, carry):
        @pl.when(jnp.logical_and(i >= 1, i < 1 + CHUNKS))
        def _():
            after_z(i - 1)

        @pl.when(jnp.logical_and(i >= 3, i < 3 + CHUNKS))
        def _():
            after_x(i - 3)

        @pl.when(i >= 5)
        def _():
            after_y(i - 5)
            finish(i - 5)

        @pl.when(i < CHUNKS)
        def _():
            local_part(i)

        return carry

    lax.fori_loop(0, 5 + CHUNKS, step, 0)

    for copies in (b_copies, c_copies):
        for copy in copies:
            copy.wait_send()
    tx_copy.wait_send()
    for d in (1, 2, 3):
        tz_copy(d).wait_send()
        ty_copy(d).wait_send()

    def drain(c, carry):
        for d in (1, 2, 3):
            z_copy(c, d).wait_send()

            @pl.when(y + d < 4)
            def _():
                y_copy(c, d).wait_send()

        x_copy(c).wait_send()
        out_copy(c).wait()
        return carry

    lax.fori_loop(0, CHUNKS, drain, 0)


def on_device(
    mixer_input, write_map, read_map, step_size, log_decay, skip_gain, level_table, level_index
):
    vmem, hbm = pl.BlockSpec(memory_space=pltpu.VMEM), pl.BlockSpec(memory_space=pl.ANY)
    dma = pltpu.SemaphoreType.DMA
    columns = HEADS * 64
    return pl.pallas_call(
        kernel,
        out_shape=jax.ShapeDtypeStruct((TOKENS, columns), BF),
        in_specs=[hbm] + [vmem] * 8,
        out_specs=hbm,
        scratch_shapes=[
            pltpu.VMEM((CHUNKS, TOKENS, WIDE), BF),
            pltpu.VMEM((STATE, TOKENS), BF),
            pltpu.VMEM((STATE, TOKENS), BF),
            pltpu.VMEM((32, TOKENS), F32),
            pltpu.VMEM((32, TOKENS), F32),
            pltpu.VMEM((16, TOKENS), F32),
            pltpu.VMEM((8, SUB), F32),
            pltpu.VMEM((SUB, SUB), F32),
            pltpu.VMEM((CHUNKS, 8, TOKENS), F32),
            pltpu.VMEM((TOKENS, SUB), F32),
            pltpu.VMEM((TOKENS, 2 * SUB), BF),
            pltpu.VMEM((NSUB, SUB), F32),
            pltpu.VMEM((SUB, SUB), BF),
            pltpu.VMEM((CHUNKS, 64, WIDE), F32),
            pltpu.VMEM((4, CHUNKS, 2 * SUB, WIDE), BF),
            pltpu.VMEM((30, STATE, WIDE), F32),
            pltpu.VMEM((CHUNKS, len(LOCAL) * STATE, WIDE), BF),
            pltpu.VMEM((NSUB, SUB, SUB), F32),
            pltpu.VMEM((TOKENS, LEVELS * STATE), BF),
            pltpu.VMEM((CHUNKS, TOKENS, WIDE), F32),
            pltpu.VMEM((CHUNKS, TOKENS, WIDE), BF),
            pltpu.VMEM((CHUNKS, 4, STATE, WIDE), BF),
            pltpu.VMEM((CHUNKS, 2, STATE, WIDE), BF),
            pltpu.VMEM((CHUNKS, 4, STATE, WIDE), BF),
            pltpu.VMEM((CHUNKS, 5 * STATE, WIDE), BF),
            pltpu.VMEM((4, 8, SUB), F32),
            pltpu.VMEM((2, 8, SUB), F32),
            pltpu.VMEM((4, 8, SUB), F32),
            pltpu.VMEM((16, SUB), F32),
            pltpu.VMEM((CHUNKS, 16, WIDE), F32),
            dma((3,)), dma((3,)), dma((3,)), dma((3,)),
            dma((3,)), dma((3,)), dma(()), dma(()), dma((3,)), dma((3,)),
            dma((CHUNKS, 3)), dma((CHUNKS, 3)), dma((CHUNKS,)), dma((CHUNKS,)),
            dma((CHUNKS, 3)), dma((CHUNKS, 3)), dma((CHUNKS,)), dma((CHUNKS,)),
        ],
        compiler_params=pltpu.CompilerParams(
            collective_id=0, has_side_effects=True, vmem_limit_bytes=60 * 2**20
        ),
    )(
        mixer_input,
        write_map.T,
        read_map.T,
        step_size,
        log_decay,
        skip_gain.reshape(1, HEADS),
        level_table.T,
        level_index,
        jnp.asarray(range_matrix(), BF),
    )


def solution(mesh):
    placed = (
        P("seq", "head"),
        P("seq", "head"),
        P("seq", "head"),
        P("head", "seq"),
        P("head", "seq"),
        P("head"),
        P(),
        P(None, "seq"),
    )
    return jax.shard_map(
        on_device, mesh=mesh, in_specs=placed, out_specs=P("seq", "head"), check_vma=False
    )
```

```python
import math

import jax
import jax.numpy as jnp
import numpy as np
from jax import lax
from jax.experimental import pallas as pl
from jax.experimental.pallas import tpu as pltpu
from jax.sharding import PartitionSpec as P

SUB = 128
NSUB = 16
TOKENS = SUB * NSUB
HEADS = 20
WIDE = 256
CHUNKS = 5
STATE = 128
SHARE = 32
LEVELS = 9
TABLE = 8
LOG2E = math.log2(math.e)
MESH = pl.DeviceIdType.MESH
BF = jnp.bfloat16
F32 = jnp.float32

COL_MIX, COL_END, COL_OUT, COL_FAR, COL_LEVEL, COL_SUM = 0, 24, 48, 72, 96, 104
LEVEL_LANE = [COL_LEVEL + i for i in range(8)] + [20]
SPREAD_BASE = (COL_END, COL_OUT, COL_FAR, COL_SUM)


def range_rows():
    rows = {}

    def row(lo, hi):
        return rows.setdefault((lo, hi), len(rows))

    merge = {}
    for i in range(4):
        for k in range(NSUB >> (i + 1)):
            merge[i, k] = row((2 * k + 1) << i, (2 * k + 2) << i)
    scale = {}
    for j in range(NSUB):
        bits = [i for i in range(4) if j >> i & 1]
        for i in bits[1:]:
            scale[j, i] = row((j >> i) << i, j)
    total = row(0, NSUB)
    return rows, merge, scale, total


ROWS, MERGE, SCALE, TOTAL = range_rows()
SKIP_ROW = 63
LOCAL = [(j, i) for j in range(NSUB) for i in range(4) if j >> i & 1]
LOCAL_AT = {pair: n for n, pair in enumerate(LOCAL)}


def range_matrix():
    w = np.zeros((64, 128), np.float32)
    for (lo, hi), r in ROWS.items():
        for part in range(3):
            w[r, part * NSUB + lo : part * NSUB + hi] = 1.0
    return w


def dot(a, b):
    return jnp.dot(a, b, preferred_element_type=F32)


def split2(v):
    hi = v.astype(BF)
    return hi, (v - hi.astype(F32)).astype(BF)


def split3(v):
    hi = v.astype(BF)
    rest = v - hi.astype(F32)
    mid = rest.astype(BF)
    return hi, mid, (rest - mid.astype(F32)).astype(BF)


def kernel(
    x_hbm, b_own, c_own, step_in, decay_in, index_in, skip_in, table_in, ranges_in,
    out_ref,
    x_s, b_t, c_t, ld_in, st_in, ld_s, st_s, ix_s, lw_s, tab_s, m_s, m2_s, rv_s, colg, colhl, tots, tots3,
    rexp, spread, take, lift, tree, loc, scm, qs, wide_s, decay_s, part, zbuf, xbuf, ybuf, rbuf,
    tz, tx, ty, secc, secz, secw,
    bs, br, cs, cr, tzs, tzr, txs, txr, tys, tyr, zs, zr, xs, xr, ys, yr, ins, small,
):
    seq = lax.axis_index("seq")
    me = lax.axis_index("head")
    z, xh, y = seq % 4, (seq // 4) % 2, seq // 8
    sib = me // 2 * 2 + (me + 1) % 2
    opp = (me + 2) % 4

    def at(z=z, xh=xh, y=y, h=me):
        return {"seq": (y * 2 + xh) * 4 + z, "head": h}

    def remote(src, dst, ssem, rsem, where):
        return pltpu.make_async_remote_copy(
            src_ref=src, dst_ref=dst, send_sem=ssem, recv_sem=rsem,
            device_id=where, device_id_type=MESH,
        )

    def cols(j):
        return pl.ds(pl.multiple_of(j * SUB, SUB), SUB)

    own_rows = pl.ds(pl.multiple_of(me * SHARE, SHARE), SHARE)
    opp_rows = pl.ds(pl.multiple_of(opp * SHARE, SHARE), SHARE)
    ld_s[16:32, :] = jnp.zeros((16, TOKENS), F32)
    st_s[16:32, :] = jnp.zeros((16, TOKENS), F32)
    inputs = [
        pltpu.make_async_copy(b_own, b_t.at[own_rows], small.at[0]),
        pltpu.make_async_copy(c_own, c_t.at[own_rows], small.at[1]),
        pltpu.make_async_copy(decay_in, ld_in, small.at[2]),
        pltpu.make_async_copy(step_in, st_in, small.at[3]),
        pltpu.make_async_copy(index_in, ix_s, small.at[4]),
    ]
    for copy in inputs:
        copy.start()

    peers = [at(h=sib), at(h=opp)]
    peers += [at(z=(z + d) % 4) for d in (1, 2, 3)]
    peers += [at(xh=1 - xh)]
    peers += [at(y=(y + d) % 4) for d in (1, 2, 3)]
    barrier = pltpu.get_barrier_semaphore()
    for p in peers:
        pl.semaphore_signal(barrier, inc=1, device_id=p, device_id_type=MESH)

    def x_in(c):
        return pltpu.make_async_copy(
            x_hbm.at[:, pl.ds(pl.multiple_of(c * WIDE, WIDE), WIDE)], x_s.at[c], ins.at[c]
        )

    for c in range(CHUNKS):
        x_in(c).start()


    def share_copies(buf, ss, rs):
        own = buf.at[own_rows]
        far = buf.at[opp_rows]
        return (
            remote(own, own, ss.at[0], rs.at[0], at(h=opp)),
            remote(own, own, ss.at[1], rs.at[1], at(h=sib)),
            remote(far, far, ss.at[2], rs.at[2], at(h=sib)),
        )

    b_copies = share_copies(b_t, bs, br)
    c_copies = share_copies(c_t, cs, cr)
    inputs[0].wait()
    pl.semaphore_wait(barrier, len(peers))
    for k in (0, 1):
        b_copies[k].start()

    for copy in inputs[2:]:
        copy.wait()
    ld_s[0:HEADS, :] = ld_in[...]
    st_s[0:HEADS, :] = st_in[...]
    tab_s[...] = jnp.zeros_like(tab_s)
    tab_s[:, 0:LEVELS] = table_in[...]
    tab_t = tab_s[...].T
    lw_s[...] = jnp.ones_like(lw_s)
    weight = jnp.zeros((LEVELS, TOKENS), F32)
    index = ix_s[...]
    for e in range(TABLE):
        weight = weight + jnp.where(index == e, tab_t[0:LEVELS, e : e + 1], 0.0)
    lw_s[0:LEVELS, :] = weight

    lanes3 = lax.broadcasted_iota(jnp.int32, (3 * SUB, SUB), 1)
    rows3 = lax.broadcasted_iota(jnp.int32, (3 * SUB, SUB), 0) & (SUB - 1)
    upper = jnp.where(rows3 <= lanes3, 1.0, 0.0).astype(BF)

    m2_s[...] = jnp.zeros_like(m2_s)

    def prepare(j, off):
        here = cols(j)
        hi, mid, lo = split3(ld_s[:, here])
        d = dot(jnp.concatenate([hi, mid, lo], axis=1), upper)[0:24]
        total = jnp.broadcast_to(d[:, SUB - 1 : SUB], (24, SUB))
        log_step = jnp.log(st_s[0:24, here]) * LOG2E
        lw = lw_s[:, here]
        d2 = d * LOG2E
        rv = d2 - log_step
        for c in range(CHUNKS):
            rv_s[c, 0:4, here] = rv[4 * c : 4 * c + 4]
        for n, piece in enumerate(split3(d2 + jnp.log(lw[0:1]) * LOG2E)):
            m2_s[24 * n : 24 * n + 24, :] = piece.astype(F32)
        colg[here, :] = m2_s[...].T.astype(BF)
        m_s[0:24, :] = jnp.zeros((24, SUB), F32)
        m_s[20:21, :] = lw[8:9]
        m_s[COL_END : COL_END + 24, :] = jnp.exp2((total - d) * LOG2E + log_step)
        m_s[COL_OUT : COL_OUT + 24, :] = jnp.exp2(d2)
        m_s[COL_FAR : COL_FAR + 24, :] = jnp.exp2((d + off) * LOG2E)
        m_s[COL_LEVEL : COL_LEVEL + 8, :] = lw[0:8]
        m_s[COL_SUM : COL_SUM + 24, :] = d
        mt = m_s[...].T
        hi2, lo2 = split2(mt)
        colhl[here, 0:SUB] = hi2
        colhl[here, SUB : 2 * SUB] = lo2
        tots[pl.ds(j, 1), :] = mt[SUB - 1 : SUB, :]
        return off + total

    lax.fori_loop(0, NSUB, prepare, jnp.zeros((24, SUB), F32), unroll=4)

    k_at = lax.broadcasted_iota(jnp.int32, (2 * SUB, WIDE), 0) & (SUB - 1)
    head_at = k_at - (lax.broadcasted_iota(jnp.int32, (2 * SUB, WIDE), 1) >> 6)

    row_of = lax.broadcasted_iota(jnp.int32, (SUB, 4 * SUB), 0)
    head_of = jnp.where(row_of < 24, row_of, jnp.where(row_of < 48, row_of - 24, row_of - 48))
    head_of = jnp.where(row_of < 72, head_of, 4096)
    taken = head_of - (lax.broadcasted_iota(jnp.int32, (SUB, 4 * SUB), 1) >> 7)
    lane_in = lax.broadcasted_iota(jnp.int32, (2 * SUB, SUB), 0) & (SUB - 1)
    for i, lane in enumerate(LEVEL_LANE):
        lift[:, i * SUB : (i + 1) * SUB] = jnp.where(lane_in == lane, 1.0, 0.0).astype(BF)

    def build(c, carry):
        for g, base in enumerate(SPREAD_BASE):
            spread[g, c] = jnp.where(head_at == base + 4 * c, 1.0, 0.0).astype(BF)
        take[c] = jnp.where(taken == 4 * c, 1.0, 0.0).astype(BF)
        return carry

    lax.fori_loop(0, CHUNKS, build, 0)

    tots3[...] = jnp.zeros_like(tots3)
    for n, piece in enumerate(split3(tots[...])):
        tots3[n * NSUB : (n + 1) * NSUB, :] = piece
    range_log = dot(ranges_in[...], tots3[...])
    lane_at = lax.broadcasted_iota(jnp.int32, (64, SUB), 1)
    range_log = jnp.where(lane_at >= COL_SUM, range_log, 0.0)
    own_total = jnp.broadcast_to(range_log[TOTAL : TOTAL + 1], (8, SUB))
    tz[z] = own_total

    def tz_copy(d):
        return remote(tz.at[z], tz.at[z], tzs.at[d - 1], tzr.at[d - 1], at(z=(z + d) % 4))

    def tz_arrival(d):
        k = (z - d) % 4
        return remote(tz.at[k], tz.at[k], tzs.at[d - 1], tzr.at[d - 1], at(z=k))

    for d in (1, 2, 3):
        tz_copy(d).start()

    tab_s[...] = jnp.zeros_like(tab_s)
    tab_s[0:1, 0:HEADS] = skip_in[...]
    skip_row = pltpu.roll(tab_s[...], COL_SUM, 1)[0:1]
    row_at = lax.broadcasted_iota(jnp.int32, (64, SUB), 0)
    factor = jnp.where(row_at == SKIP_ROW, skip_row, jnp.exp(range_log))
    factor = jnp.concatenate(split2(factor), axis=1)

    def spread_rows(c, carry):
        rexp[c] = dot(factor, spread[3, c])
        return carry

    lax.fori_loop(0, CHUNKS, spread_rows, 0)

    b_copies[0].wait_recv()
    b_copies[2].start()
    inputs[1].wait()
    for k in (0, 1):
        c_copies[k].start()
    b_copies[1].wait_recv()
    b_copies[2].wait_recv()

    for d in (1, 2, 3):
        tz_arrival(d).wait_recv()
    far_t = [tz[k, 0:1] for k in range(4)]
    tx[xh] = jnp.broadcast_to(far_t[0] + far_t[1] + far_t[2] + far_t[3], (8, SUB))
    tx_copy = remote(tx.at[xh], tx.at[xh], txs, txr, at(xh=1 - xh))
    tx_copy.start()

    def ty_copy(d):
        return remote(ty.at[y], ty.at[y], tys.at[d - 1], tyr.at[d - 1], at(y=(y + d) % 4))

    def ty_arrival(d):
        k = (y - d) % 4
        return remote(ty.at[k], ty.at[k], tys.at[d - 1], tyr.at[d - 1], at(y=k))

    def z_copy(c, d):
        return remote(
            zbuf.at[c, z], zbuf.at[c, z], zs.at[c, d - 1], zr.at[c, d - 1], at(z=(z + d) % 4)
        )

    def z_arrival(c, d):
        k = (z - d) % 4
        return remote(zbuf.at[c, k], zbuf.at[c, k], zs.at[c, d - 1], zr.at[c, d - 1], at(z=k))

    first = {0: 0, 1: 16, 2: 24, 3: 28}

    def states(c, carry):
        x_in(c).wait()

        @pl.when(c == 3)
        def _():
            c_copies[0].wait_recv()
            c_copies[2].start()
            tx_copy.wait_recv()
            ty[y] = jnp.broadcast_to(tx[0, 0:1] + tx[1, 0:1], (8, SUB))
            for d in (1, 2, 3):
                ty_copy(d).start()

        def one(j, carry):
            here = cols(j)
            end = dot(colhl[here, :], spread[0, c])
            scaled = (x_s[c, here, :].astype(F32) * end).astype(BF)
            tree[j] = dot(b_t[:, here], scaled)
            return carry

        lax.fori_loop(0, NSUB, one, 0, unroll=True)
        for i in range(4):
            for k in range(NSUB >> (i + 1)):
                r = MERGE[i, k]
                merged = (
                    rexp[c, r : r + 1, :] * tree[first[i] + 2 * k] + tree[first[i] + 2 * k + 1]
                )
                if i < 3:
                    tree[first[i + 1] + k] = merged
                else:
                    zbuf[c, z] = merged.astype(BF)
        for d in (1, 2, 3):
            z_copy(c, d).start()
        for (j, i), n in LOCAL_AT.items():
            value = tree[first[i] + (j >> i) - 1]
            if (j, i) in SCALE:
                r = SCALE[j, i]
                value = rexp[c, r : r + 1, :] * value
            loc[c, n * STATE : (n + 1) * STATE, :] = value.astype(BF)
        return carry

    lax.fori_loop(0, CHUNKS, states, 0)

    c_copies[1].wait_recv()
    c_copies[2].wait_recv()
    causal = lax.broadcasted_iota(jnp.int32, (SUB, SUB), 0) >= lax.broadcasted_iota(
        jnp.int32, (SUB, SUB), 1
    )

    def queries(j, carry):
        here = cols(j)
        c_rows = c_t[:, here].astype(F32).T
        scm[j] = jnp.where(causal, dot(c_rows.astype(BF), b_t[:, here]), 0.0)
        level = dot(colhl[here, :], lift[...])
        for i in range(LEVELS):
            at_level = slice(i * STATE, (i + 1) * STATE)
            qs[here, at_level] = (level[:, at_level] * c_rows).astype(BF)
        return carry

    lax.fori_loop(0, NSUB, queries, 0, unroll=4)

    t0, t1, t2, t3 = far_t

    def only(flag, row):
        return jnp.where(flag, row, 0.0)

    run2 = only(z > 0, t0) + only(z > 1, t1) + only(z > 2, t2)
    low_run = only(z == 3, t2)
    upper_z, upper_y = z >= 2, y >= 2

    def spread_weights(weights, where_to):
        for n, w in enumerate(weights):
            secc[n : n + 1, :] = w
        compact = jnp.concatenate(split2(secc[...]), axis=1)

        def spread_one(c, carry):
            where_to[c] = dot(compact, spread[3, c])
            return carry

        lax.fori_loop(0, CHUNKS, spread_one, 0, unroll=True)

    secc[...] = jnp.zeros_like(secc)
    spread_weights(
        [
            jnp.exp(t1 + t2 + t3),
            jnp.exp(t2 + t3),
            jnp.exp(t3),
            only(upper_z, jnp.exp(t1 + low_run)),
            only(upper_z, jnp.exp(low_run)),
        ],
        secz,
    )

    def later_weights():
        for d in (1, 2, 3):
            ty_arrival(d).wait_recv()
        u0, u1 = tx[0, 0:1], tx[1, 0:1]
        v1, v2 = ty[1, 0:1], ty[2, 0:1]
        run3 = run2 + only(xh == 1, u0)
        run4 = run3 + only(y == 3, v2)
        spread_weights(
            [
                only(xh == 1, jnp.exp(run2)),
                jnp.exp(u1),
                jnp.exp(run3),
                jnp.exp(v1 + run4),
                jnp.exp(run4),
            ],
            secw,
        )

    def x_copy(c):
        return remote(xbuf.at[c, xh], xbuf.at[c, xh], xs.at[c], xr.at[c], at(xh=1 - xh))

    def x_arrival(c):
        k = 1 - xh
        return remote(xbuf.at[c, k], xbuf.at[c, k], xs.at[c], xr.at[c], at(xh=k))

    def y_copy(c, d):
        return remote(
            ybuf.at[c, y], ybuf.at[c, y], ys.at[c, d - 1], yr.at[c, d - 1], at(y=(y + d) % 4)
        )

    def y_arrival(c, d):
        k = (y - d) % 4
        return remote(ybuf.at[c, k], ybuf.at[c, k], ys.at[c, d - 1], yr.at[c, d - 1], at(y=k))

    def after_z(c):
        for d in (1, 2, 3):
            z_arrival(c, d).wait_recv()
        w = [secz[c, n : n + 1, :] for n in range(5)]
        s = [zbuf[c, k].astype(F32) for k in range(4)]
        xbuf[c, xh] = (w[0] * s[0] + w[1] * s[1] + (w[2] * s[2] + s[3])).astype(BF)
        x_copy(c).start()
        rbuf[c, 0:STATE, :] = jnp.where(
            z % 2 == 1, zbuf[c, jnp.maximum(z - 1, 0)].astype(F32), 0.0
        ).astype(BF)
        rbuf[c, STATE : 2 * STATE, :] = (w[3] * s[0] + w[4] * s[1]).astype(BF)

    def after_x(c):
        x_arrival(c).wait_recv()
        s = [xbuf[c, k].astype(F32) for k in range(2)]
        ybuf[c, y] = (secw[c, 1:2, :] * s[0] + s[1]).astype(BF)
        for d in (1, 2, 3):

            @pl.when(y + d < 4)
            def _():
                y_copy(c, d).start()

        rbuf[c, 2 * STATE : 3 * STATE, :] = (secw[c, 0:1, :] * s[0]).astype(BF)

    def after_y(c):
        for d in (1, 2, 3):

            @pl.when(y >= d)
            def _():
                y_arrival(c, d).wait_recv()

        near = secw[c, 2:3, :] * ybuf[c, jnp.maximum(y - 1, 0)].astype(F32)
        rbuf[c, 3 * STATE : 4 * STATE, :] = jnp.where(y % 2 == 1, near, 0.0).astype(BF)
        wide = secw[c, 3:4, :] * ybuf[c, 0].astype(F32) + secw[c, 4:5, :] * ybuf[c, 1].astype(F32)
        rbuf[c, 4 * STATE : 5 * STATE, :] = jnp.where(upper_y, wide, 0.0).astype(BF)

    low_half = lax.broadcasted_iota(jnp.int32, (SUB, SUB), 1) < 64

    def local_part(c):
        skip = rexp[c, SKIP_ROW : SKIP_ROW + 1, :]
        for j in range(NSUB):
            here = pl.ds(j * SUB, SUB)
            if j % (NSUB // 2) == 0:
                many = pl.ds(j * SUB, TOKENS // 2)
                wide_s[...] = dot(colg[many, :], take[c])
                decay_s[...] = dot(colhl[many, :], spread[1, c])
            now = pl.ds(j % (NSUB // 2) * SUB, SUB)
            masked = scm[j]
            xt = x_s[c, here, :]
            xf = xt.astype(F32)
            halves = []
            for pair in range(2):
                mixes = []
                for k in (2 * pair, 2 * pair + 1):
                    gap = wide_s[now, k * SUB : (k + 1) * SUB] - rv_s[c, k : k + 1, here]
                    mixes.append((masked * jnp.exp2(jnp.minimum(gap, 64.0))).astype(BF))
                xp = xf[:, pair * SUB : (pair + 1) * SUB]
                both = jnp.concatenate(
                    [
                        jnp.where(low_half, xp, 0.0).astype(BF),
                        jnp.where(low_half, 0.0, xp).astype(BF),
                    ],
                    axis=0,
                )
                halves.append(dot(jnp.concatenate(mixes, axis=1), both))
            result = jnp.concatenate(halves, axis=1) + skip * xf
            bits = [i for i in range(4) if j >> i & 1]
            if bits:
                q = jnp.concatenate([qs[here, i * STATE : (i + 1) * STATE] for i in bits], axis=1)
                lo = LOCAL_AT[j, bits[0]] * STATE
                near = dot(q, loc[c, lo : lo + len(bits) * STATE, :])
                result = result + decay_s[now, :] * near
            part[c, here, :] = result

    def finish(c):
        def one(j, carry):
            here = pl.ds(pl.multiple_of(j * 256, 256), 256)
            far = dot(qs[here, 4 * STATE : 9 * STATE], rbuf[c])
            result = part[c, here, :] + dot(colhl[here, :], spread[2, c]) * far
            out_ref[here, pl.ds(pl.multiple_of(c * WIDE, WIDE), WIDE)] = result.astype(BF)
            return carry

        lax.fori_loop(0, TOKENS // 256, one, 0, unroll=True)

    def step(i, carry):
        @pl.when(i < CHUNKS)
        def _():
            after_z(i)

        @pl.when(i == 1)
        def _():
            later_weights()

        @pl.when(jnp.logical_and(i >= 2, i < 2 + CHUNKS))
        def _():
            after_x(i - 2)

        @pl.when(i >= 4)
        def _():
            after_y(i - 4)
            finish(i - 4)

        @pl.when(i < CHUNKS)
        def _():
            local_part(i)

        return carry

    lax.fori_loop(0, 4 + CHUNKS, step, 0)

    for copies in (b_copies, c_copies):
        for copy in copies:
            copy.wait_send()
    tx_copy.wait_send()
    for d in (1, 2, 3):
        tz_copy(d).wait_send()
        ty_copy(d).wait_send()

    def drain(c, carry):
        for d in (1, 2, 3):
            z_copy(c, d).wait_send()

            @pl.when(y + d < 4)
            def _():
                y_copy(c, d).wait_send()

        x_copy(c).wait_send()
        return carry

    lax.fori_loop(0, CHUNKS, drain, 0)


def on_device(
    mixer_input, write_map, read_map, step_size, log_decay, skip_gain, level_table, level_index
):
    vmem, hbm = pl.BlockSpec(memory_space=pltpu.VMEM), pl.BlockSpec(memory_space=pl.ANY)
    dma = pltpu.SemaphoreType.DMA
    columns = HEADS * 64
    return pl.pallas_call(
        kernel,
        out_shape=pltpu.VMEM((TOKENS, columns), BF),
        in_specs=[hbm] * 6 + [vmem] * 3,
        out_specs=vmem,
        scratch_shapes=[
            pltpu.VMEM((CHUNKS, TOKENS, WIDE), BF),
            pltpu.VMEM((STATE, TOKENS), BF),
            pltpu.VMEM((STATE, TOKENS), BF),
            pltpu.VMEM((HEADS, TOKENS), F32),
            pltpu.VMEM((HEADS, TOKENS), F32),
            pltpu.VMEM((32, TOKENS), F32),
            pltpu.VMEM((32, TOKENS), F32),
            pltpu.VMEM((LEVELS, TOKENS), jnp.int32),
            pltpu.VMEM((16, TOKENS), F32),
            pltpu.VMEM((8, SUB), F32),
            pltpu.VMEM((SUB, SUB), F32),
            pltpu.VMEM((SUB, SUB), F32),
            pltpu.VMEM((CHUNKS, 8, TOKENS), F32),
            pltpu.VMEM((TOKENS, SUB), BF),
            pltpu.VMEM((TOKENS, 2 * SUB), BF),
            pltpu.VMEM((NSUB, SUB), F32),
            pltpu.VMEM((SUB, SUB), BF),
            pltpu.VMEM((CHUNKS, 64, WIDE), F32),
            pltpu.VMEM((4, CHUNKS, 2 * SUB, WIDE), BF),
            pltpu.VMEM((CHUNKS, SUB, 4 * SUB), BF),
            pltpu.VMEM((2 * SUB, LEVELS * SUB), BF),
            pltpu.VMEM((30, STATE, WIDE), F32),
            pltpu.VMEM((CHUNKS, len(LOCAL) * STATE, WIDE), BF),
            pltpu.VMEM((NSUB, SUB, SUB), F32),
            pltpu.VMEM((TOKENS, LEVELS * STATE), BF),
            pltpu.VMEM((TOKENS // 2, 4 * SUB), F32),
            pltpu.VMEM((TOKENS // 2, WIDE), F32),
            pltpu.VMEM((CHUNKS, TOKENS, WIDE), F32),
            pltpu.VMEM((CHUNKS, 4, STATE, WIDE), BF),
            pltpu.VMEM((CHUNKS, 2, STATE, WIDE), BF),
            pltpu.VMEM((CHUNKS, 4, STATE, WIDE), BF),
            pltpu.VMEM((CHUNKS, 5 * STATE, WIDE), BF),
            pltpu.VMEM((4, 8, SUB), F32),
            pltpu.VMEM((2, 8, SUB), F32),
            pltpu.VMEM((4, 8, SUB), F32),
            pltpu.VMEM((16, SUB), F32),
            pltpu.VMEM((CHUNKS, 16, WIDE), F32),
            pltpu.VMEM((CHUNKS, 16, WIDE), F32),
            dma((3,)), dma((3,)), dma((3,)), dma((3,)),
            dma((3,)), dma((3,)), dma(()), dma(()), dma((3,)), dma((3,)),
            dma((CHUNKS, 3)), dma((CHUNKS, 3)), dma((CHUNKS,)), dma((CHUNKS,)),
            dma((CHUNKS, 3)), dma((CHUNKS, 3)), dma((CHUNKS,)), dma((5,)),
        ],
        compiler_params=pltpu.CompilerParams(
            collective_id=0, has_side_effects=True, vmem_limit_bytes=54 * 2**20
        ),
    )(
        mixer_input,
        write_map.T,
        read_map.T,
        step_size,
        log_decay,
        level_index,
        skip_gain.reshape(1, HEADS),
        level_table.T,
        jnp.asarray(range_matrix(), BF),
    )


def solution(mesh):
    placed = (
        P("seq", "head"),
        P("seq", "head"),
        P("seq", "head"),
        P("head", "seq"),
        P("head", "seq"),
        P("head"),
        P(),
        P(None, "seq"),
    )
    return jax.shard_map(
        on_device, mesh=mesh, in_specs=placed, out_specs=P("seq", "head"), check_vma=False
    )
```

```python
import math

import jax
import jax.numpy as jnp
import numpy as np
from jax import lax
from jax.experimental import pallas as pl
from jax.experimental.pallas import tpu as pltpu
from jax.sharding import PartitionSpec as P

SUB = 128
NSUB = 16
TOKENS = SUB * NSUB
HEADS = 20
WIDE = 256
CHUNKS = 5
STATE = 128
SHARE = 32
LEVELS = 9
TABLE = 8
LOG2E = math.log2(math.e)
MESH = pl.DeviceIdType.MESH
BF = jnp.bfloat16
F32 = jnp.float32

COL_MIX, COL_END, COL_OUT, COL_FAR, COL_LEVEL, COL_SUM = 0, 24, 48, 72, 96, 104
LEVEL_LANE = [COL_LEVEL + i for i in range(8)] + [20]
SPREAD_BASE = (COL_END, COL_OUT, COL_FAR, COL_SUM)


def range_rows():
    rows = {}

    def row(lo, hi):
        return rows.setdefault((lo, hi), len(rows))

    merge = {}
    for i in range(4):
        for k in range(NSUB >> (i + 1)):
            merge[i, k] = row((2 * k + 1) << i, (2 * k + 2) << i)
    scale = {}
    for j in range(NSUB):
        bits = [i for i in range(4) if j >> i & 1]
        for i in bits[1:]:
            scale[j, i] = row((j >> i) << i, j)
    total = row(0, NSUB)
    return rows, merge, scale, total


ROWS, MERGE, SCALE, TOTAL = range_rows()
SKIP_ROW = 63
LOCAL = [(j, i) for j in range(NSUB) for i in range(4) if j >> i & 1]
LOCAL_AT = {pair: n for n, pair in enumerate(LOCAL)}


def range_matrix():
    w = np.zeros((64, 128), np.float32)
    for (lo, hi), r in ROWS.items():
        for part in range(3):
            w[r, part * NSUB + lo : part * NSUB + hi] = 1.0
    return w


def dot(a, b):
    return jnp.dot(a, b, preferred_element_type=F32)


def split2(v):
    hi = v.astype(BF)
    return hi, (v - hi.astype(F32)).astype(BF)


def split3(v):
    hi = v.astype(BF)
    rest = v - hi.astype(F32)
    mid = rest.astype(BF)
    return hi, mid, (rest - mid.astype(F32)).astype(BF)


def kernel(
    x_hbm, b_own, c_own, step_in, decay_in, index_in, skip_in, table_in, ranges_in,
    out_ref,
    x_s, b_t, c_t, ld_in, st_in, ld_s, st_s, ix_s, lw_s, tab_s, m_s, m2_s, rv_s, colg, colhl, tots, tots3,
    rexp, spread, take, lift, tree, loc, scm, qs, wide_s, decay_s, part, zbuf, xbuf, ybuf, rbuf,
    tz, tx, ty, secc, secz, secw,
    bs, br, cs, cr, tzs, tzr, txs, txr, tys, tyr, zs, zr, xs, xr, ys, yr, ins, small,
):
    seq = lax.axis_index("seq")
    me = lax.axis_index("head")
    z, xh, y = seq % 4, (seq // 4) % 2, seq // 8
    sib = me // 2 * 2 + (me + 1) % 2
    opp = (me + 2) % 4

    def at(z=z, xh=xh, y=y, h=me):
        return {"seq": (y * 2 + xh) * 4 + z, "head": h}

    def remote(src, dst, ssem, rsem, where):
        return pltpu.make_async_remote_copy(
            src_ref=src, dst_ref=dst, send_sem=ssem, recv_sem=rsem,
            device_id=where, device_id_type=MESH,
        )

    def cols(j):
        return pl.ds(pl.multiple_of(j * SUB, SUB), SUB)

    own_rows = pl.ds(pl.multiple_of(me * SHARE, SHARE), SHARE)
    opp_rows = pl.ds(pl.multiple_of(opp * SHARE, SHARE), SHARE)
    ld_s[16:32, :] = jnp.zeros((16, TOKENS), F32)
    st_s[16:32, :] = jnp.zeros((16, TOKENS), F32)
    inputs = [
        pltpu.make_async_copy(b_own, b_t.at[own_rows], small.at[0]),
        pltpu.make_async_copy(c_own, c_t.at[own_rows], small.at[1]),
        pltpu.make_async_copy(decay_in, ld_in, small.at[2]),
        pltpu.make_async_copy(step_in, st_in, small.at[3]),
        pltpu.make_async_copy(index_in, ix_s, small.at[4]),
    ]
    for copy in inputs:
        copy.start()

    peers = [at(h=sib), at(h=opp)]
    peers += [at(z=(z + d) % 4) for d in (1, 2, 3)]
    peers += [at(xh=1 - xh)]
    peers += [at(y=(y + d) % 4) for d in (1, 2, 3)]
    barrier = pltpu.get_barrier_semaphore()
    for p in peers:
        pl.semaphore_signal(barrier, inc=1, device_id=p, device_id_type=MESH)

    def x_in(c):
        return pltpu.make_async_copy(
            x_hbm.at[:, pl.ds(pl.multiple_of(c * WIDE, WIDE), WIDE)], x_s.at[c], ins.at[c]
        )

    for c in range(CHUNKS):
        x_in(c).start()


    def share_copies(buf, ss, rs):
        own = buf.at[own_rows]
        far = buf.at[opp_rows]
        return (
            remote(own, own, ss.at[0], rs.at[0], at(h=opp)),
            remote(own, own, ss.at[1], rs.at[1], at(h=sib)),
            remote(far, far, ss.at[2], rs.at[2], at(h=sib)),
        )

    b_copies = share_copies(b_t, bs, br)
    c_copies = share_copies(c_t, cs, cr)
    inputs[0].wait()
    pl.semaphore_wait(barrier, len(peers))
    for k in (0, 1):
        b_copies[k].start()

    for copy in inputs[2:]:
        copy.wait()
    ld_s[0:HEADS, :] = ld_in[...]
    st_s[0:HEADS, :] = st_in[...]
    tab_s[...] = jnp.zeros_like(tab_s)
    tab_s[:, 0:LEVELS] = table_in[...]
    tab_t = tab_s[...].T
    lw_s[...] = jnp.ones_like(lw_s)
    weight = jnp.zeros((LEVELS, TOKENS), F32)
    index = ix_s[...]
    for e in range(TABLE):
        weight = weight + jnp.where(index == e, tab_t[0:LEVELS, e : e + 1], 0.0)
    lw_s[0:LEVELS, :] = weight

    lanes3 = lax.broadcasted_iota(jnp.int32, (3 * SUB, SUB), 1)
    rows3 = lax.broadcasted_iota(jnp.int32, (3 * SUB, SUB), 0) & (SUB - 1)
    upper = jnp.where(rows3 <= lanes3, 1.0, 0.0).astype(BF)

    m2_s[...] = jnp.zeros_like(m2_s)

    def prepare(j, off):
        here = cols(j)
        hi, mid, lo = split3(ld_s[:, here])
        d = dot(jnp.concatenate([hi, mid, lo], axis=1), upper)[0:24]
        total = jnp.broadcast_to(d[:, SUB - 1 : SUB], (24, SUB))
        log_step = jnp.log(st_s[0:24, here]) * LOG2E
        lw = lw_s[:, here]
        d2 = d * LOG2E
        rv = d2 - log_step
        for c in range(CHUNKS):
            rv_s[c, 0:4, here] = rv[4 * c : 4 * c + 4]
        for n, piece in enumerate(split3(d2 + jnp.log(lw[0:1]) * LOG2E)):
            m2_s[24 * n : 24 * n + 24, :] = piece.astype(F32)
        colg[here, :] = m2_s[...].T.astype(BF)
        m_s[0:24, :] = jnp.zeros((24, SUB), F32)
        m_s[20:21, :] = lw[8:9]
        m_s[COL_END : COL_END + 24, :] = jnp.exp2((total - d) * LOG2E + log_step)
        m_s[COL_OUT : COL_OUT + 24, :] = jnp.exp2(d2)
        m_s[COL_FAR : COL_FAR + 24, :] = jnp.exp2((d + off) * LOG2E)
        m_s[COL_LEVEL : COL_LEVEL + 8, :] = lw[0:8]
        m_s[COL_SUM : COL_SUM + 24, :] = d
        mt = m_s[...].T
        hi2, lo2 = split2(mt)
        colhl[here, 0:SUB] = hi2
        colhl[here, SUB : 2 * SUB] = lo2
        tots[pl.ds(j, 1), :] = mt[SUB - 1 : SUB, :]
        return off + total

    lax.fori_loop(0, NSUB, prepare, jnp.zeros((24, SUB), F32), unroll=4)

    k_at = lax.broadcasted_iota(jnp.int32, (2 * SUB, WIDE), 0) & (SUB - 1)
    head_at = k_at - (lax.broadcasted_iota(jnp.int32, (2 * SUB, WIDE), 1) >> 6)

    row_of = lax.broadcasted_iota(jnp.int32, (SUB, 4 * SUB), 0)
    head_of = jnp.where(row_of < 24, row_of, jnp.where(row_of < 48, row_of - 24, row_of - 48))
    head_of = jnp.where(row_of < 72, head_of, 4096)
    taken = head_of - (lax.broadcasted_iota(jnp.int32, (SUB, 4 * SUB), 1) >> 7)
    lane_in = lax.broadcasted_iota(jnp.int32, (2 * SUB, SUB), 0) & (SUB - 1)
    for i, lane in enumerate(LEVEL_LANE):
        lift[:, i * SUB : (i + 1) * SUB] = jnp.where(lane_in == lane, 1.0, 0.0).astype(BF)

    def build(c, carry):
        for g, base in enumerate(SPREAD_BASE):
            spread[g, c] = jnp.where(head_at == base + 4 * c, 1.0, 0.0).astype(BF)
        take[c] = jnp.where(taken == 4 * c, 1.0, 0.0).astype(BF)
        return carry

    lax.fori_loop(0, CHUNKS, build, 0)

    tots3[...] = jnp.zeros_like(tots3)
    for n, piece in enumerate(split3(tots[...])):
        tots3[n * NSUB : (n + 1) * NSUB, :] = piece
    range_log = dot(ranges_in[...], tots3[...])
    lane_at = lax.broadcasted_iota(jnp.int32, (64, SUB), 1)
    range_log = jnp.where(lane_at >= COL_SUM, range_log, 0.0)
    own_total = jnp.broadcast_to(range_log[TOTAL : TOTAL + 1], (8, SUB))
    tz[z] = own_total

    def tz_copy(d):
        return remote(tz.at[z], tz.at[z], tzs.at[d - 1], tzr.at[d - 1], at(z=(z + d) % 4))

    def tz_arrival(d):
        k = (z - d) % 4
        return remote(tz.at[k], tz.at[k], tzs.at[d - 1], tzr.at[d - 1], at(z=k))

    for d in (1, 2, 3):
        tz_copy(d).start()

    tab_s[...] = jnp.zeros_like(tab_s)
    tab_s[0:1, 0:HEADS] = skip_in[...]
    skip_row = pltpu.roll(tab_s[...], COL_SUM, 1)[0:1]
    row_at = lax.broadcasted_iota(jnp.int32, (64, SUB), 0)
    factor = jnp.where(row_at == SKIP_ROW, skip_row, jnp.exp(range_log))
    factor = jnp.concatenate(split2(factor), axis=1)

    def spread_rows(c, carry):
        rexp[c] = dot(factor, spread[3, c])
        return carry

    lax.fori_loop(0, CHUNKS, spread_rows, 0)

    def scale_inputs(c, carry):
        x_in(c).wait()
        for j in range(2):
            here = pl.ds(j * TOKENS // 2, TOKENS // 2)
            end = dot(colhl[here, :], spread[0, c])
            part[c, here, :] = x_s[c, here, :].astype(F32) * end
        return carry

    lax.fori_loop(0, CHUNKS, scale_inputs, 0)

    b_copies[0].wait_recv()
    b_copies[2].start()
    inputs[1].wait()
    for k in (0, 1):
        c_copies[k].start()
    b_copies[1].wait_recv()
    b_copies[2].wait_recv()

    for d in (1, 2, 3):
        tz_arrival(d).wait_recv()
    far_t = [tz[k, 0:1] for k in range(4)]
    tx[xh] = jnp.broadcast_to(far_t[0] + far_t[1] + far_t[2] + far_t[3], (8, SUB))
    tx_copy = remote(tx.at[xh], tx.at[xh], txs, txr, at(xh=1 - xh))
    tx_copy.start()

    def ty_copy(d):
        return remote(ty.at[y], ty.at[y], tys.at[d - 1], tyr.at[d - 1], at(y=(y + d) % 4))

    def ty_arrival(d):
        k = (y - d) % 4
        return remote(ty.at[k], ty.at[k], tys.at[d - 1], tyr.at[d - 1], at(y=k))

    def z_copy(c, d):
        return remote(
            zbuf.at[c, z], zbuf.at[c, z], zs.at[c, d - 1], zr.at[c, d - 1], at(z=(z + d) % 4)
        )

    def z_arrival(c, d):
        k = (z - d) % 4
        return remote(zbuf.at[c, k], zbuf.at[c, k], zs.at[c, d - 1], zr.at[c, d - 1], at(z=k))

    first = {0: 0, 1: 16, 2: 24, 3: 28}

    def states(c, carry):
        @pl.when(c == 3)
        def _():
            c_copies[0].wait_recv()
            c_copies[2].start()
            tx_copy.wait_recv()
            ty[y] = jnp.broadcast_to(tx[0, 0:1] + tx[1, 0:1], (8, SUB))
            for d in (1, 2, 3):
                ty_copy(d).start()

        def one(j, carry):
            here = cols(j)
            tree[j] = dot(b_t[:, here], part[c, here, :].astype(BF))
            return carry

        lax.fori_loop(0, NSUB, one, 0, unroll=True)
        for i in range(4):
            for k in range(NSUB >> (i + 1)):
                r = MERGE[i, k]
                merged = (
                    rexp[c, r : r + 1, :] * tree[first[i] + 2 * k] + tree[first[i] + 2 * k + 1]
                )
                if i < 3:
                    tree[first[i + 1] + k] = merged
                else:
                    zbuf[c, z] = merged.astype(BF)
        for d in (1, 2, 3):
            z_copy(c, d).start()
        for (j, i), n in LOCAL_AT.items():
            value = tree[first[i] + (j >> i) - 1]
            if (j, i) in SCALE:
                r = SCALE[j, i]
                value = rexp[c, r : r + 1, :] * value
            loc[c, n * STATE : (n + 1) * STATE, :] = value.astype(BF)
        return carry

    lax.fori_loop(0, CHUNKS, states, 0)

    c_copies[1].wait_recv()
    c_copies[2].wait_recv()
    causal = lax.broadcasted_iota(jnp.int32, (SUB, SUB), 0) >= lax.broadcasted_iota(
        jnp.int32, (SUB, SUB), 1
    )

    def queries(j, carry):
        here = cols(j)
        c_rows = c_t[:, here].astype(F32).T
        scm[j] = jnp.where(causal, dot(c_rows.astype(BF), b_t[:, here]), 0.0)
        level = dot(colhl[here, :], lift[...])
        for i in range(LEVELS):
            at_level = slice(i * STATE, (i + 1) * STATE)
            qs[here, at_level] = (level[:, at_level] * c_rows).astype(BF)
        return carry

    lax.fori_loop(0, NSUB, queries, 0, unroll=4)

    t0, t1, t2, t3 = far_t

    def only(flag, row):
        return jnp.where(flag, row, 0.0)

    run2 = only(z > 0, t0) + only(z > 1, t1) + only(z > 2, t2)
    low_run = only(z == 3, t2)
    upper_z, upper_y = z >= 2, y >= 2

    def spread_weights(weights, where_to):
        for n, w in enumerate(weights):
            secc[n : n + 1, :] = w
        compact = jnp.concatenate(split2(secc[...]), axis=1)

        def spread_one(c, carry):
            where_to[c] = dot(compact, spread[3, c])
            return carry

        lax.fori_loop(0, CHUNKS, spread_one, 0, unroll=True)

    secc[...] = jnp.zeros_like(secc)
    spread_weights(
        [
            jnp.exp(t1 + t2 + t3),
            jnp.exp(t2 + t3),
            jnp.exp(t3),
            only(upper_z, jnp.exp(t1 + low_run)),
            only(upper_z, jnp.exp(low_run)),
        ],
        secz,
    )

    def later_weights():
        for d in (1, 2, 3):
            ty_arrival(d).wait_recv()
        u0, u1 = tx[0, 0:1], tx[1, 0:1]
        v1, v2 = ty[1, 0:1], ty[2, 0:1]
        run3 = run2 + only(xh == 1, u0)
        run4 = run3 + only(y == 3, v2)
        spread_weights(
            [
                only(xh == 1, jnp.exp(run2)),
                jnp.exp(u1),
                jnp.exp(run3),
                jnp.exp(v1 + run4),
                jnp.exp(run4),
            ],
            secw,
        )

    def x_copy(c):
        return remote(xbuf.at[c, xh], xbuf.at[c, xh], xs.at[c], xr.at[c], at(xh=1 - xh))

    def x_arrival(c):
        k = 1 - xh
        return remote(xbuf.at[c, k], xbuf.at[c, k], xs.at[c], xr.at[c], at(xh=k))

    def y_copy(c, d):
        return remote(
            ybuf.at[c, y], ybuf.at[c, y], ys.at[c, d - 1], yr.at[c, d - 1], at(y=(y + d) % 4)
        )

    def y_arrival(c, d):
        k = (y - d) % 4
        return remote(ybuf.at[c, k], ybuf.at[c, k], ys.at[c, d - 1], yr.at[c, d - 1], at(y=k))

    def after_z(c):
        for d in (1, 2, 3):
            z_arrival(c, d).wait_recv()
        w = [secz[c, n : n + 1, :] for n in range(5)]
        s = [zbuf[c, k].astype(F32) for k in range(4)]
        xbuf[c, xh] = (w[0] * s[0] + w[1] * s[1] + (w[2] * s[2] + s[3])).astype(BF)
        x_copy(c).start()
        rbuf[c, 0:STATE, :] = jnp.where(
            z % 2 == 1, zbuf[c, jnp.maximum(z - 1, 0)].astype(F32), 0.0
        ).astype(BF)
        rbuf[c, STATE : 2 * STATE, :] = (w[3] * s[0] + w[4] * s[1]).astype(BF)

    def after_x(c):
        x_arrival(c).wait_recv()
        s = [xbuf[c, k].astype(F32) for k in range(2)]
        ybuf[c, y] = (secw[c, 1:2, :] * s[0] + s[1]).astype(BF)
        for d in (1, 2, 3):

            @pl.when(y + d < 4)
            def _():
                y_copy(c, d).start()

        rbuf[c, 2 * STATE : 3 * STATE, :] = (secw[c, 0:1, :] * s[0]).astype(BF)

    def after_y(c):
        for d in (1, 2, 3):

            @pl.when(y >= d)
            def _():
                y_arrival(c, d).wait_recv()

        near = secw[c, 2:3, :] * ybuf[c, jnp.maximum(y - 1, 0)].astype(F32)
        rbuf[c, 3 * STATE : 4 * STATE, :] = jnp.where(y % 2 == 1, near, 0.0).astype(BF)
        wide = secw[c, 3:4, :] * ybuf[c, 0].astype(F32) + secw[c, 4:5, :] * ybuf[c, 1].astype(F32)
        rbuf[c, 4 * STATE : 5 * STATE, :] = jnp.where(upper_y, wide, 0.0).astype(BF)

    low_half = lax.broadcasted_iota(jnp.int32, (SUB, SUB), 1) < 64

    def local_part(c):
        skip = rexp[c, SKIP_ROW : SKIP_ROW + 1, :]
        for j in range(NSUB):
            here = pl.ds(j * SUB, SUB)
            if j % (NSUB // 2) == 0:
                many = pl.ds(j * SUB, TOKENS // 2)
                wide_s[...] = dot(colg[many, :], take[c])
                decay_s[...] = dot(colhl[many, :], spread[1, c])
            now = pl.ds(j % (NSUB // 2) * SUB, SUB)
            masked = scm[j]
            xt = x_s[c, here, :]
            xf = xt.astype(F32)
            halves = []
            for pair in range(2):
                mixes = []
                for k in (2 * pair, 2 * pair + 1):
                    gap = wide_s[now, k * SUB : (k + 1) * SUB] - rv_s[c, k : k + 1, here]
                    mixes.append((masked * jnp.exp2(jnp.minimum(gap, 64.0))).astype(BF))
                xp = xf[:, pair * SUB : (pair + 1) * SUB]
                both = jnp.concatenate(
                    [
                        jnp.where(low_half, xp, 0.0).astype(BF),
                        jnp.where(low_half, 0.0, xp).astype(BF),
                    ],
                    axis=0,
                )
                halves.append(dot(jnp.concatenate(mixes, axis=1), both))
            result = jnp.concatenate(halves, axis=1) + skip * xf
            bits = [i for i in range(4) if j >> i & 1]
            if bits:
                q = jnp.concatenate([qs[here, i * STATE : (i + 1) * STATE] for i in bits], axis=1)
                lo = LOCAL_AT[j, bits[0]] * STATE
                near = dot(q, loc[c, lo : lo + len(bits) * STATE, :])
                result = result + decay_s[now, :] * near
            part[c, here, :] = result

    def finish(c):
        def one(j, carry):
            here = pl.ds(pl.multiple_of(j * 1024, 1024), 1024)
            far = dot(qs[here, 4 * STATE : 9 * STATE], rbuf[c])
            result = part[c, here, :] + dot(colhl[here, :], spread[2, c]) * far
            out_ref[here, pl.ds(pl.multiple_of(c * WIDE, WIDE), WIDE)] = result.astype(BF)
            return carry

        lax.fori_loop(0, TOKENS // 1024, one, 0, unroll=True)

    def step(i, carry):
        @pl.when(i < CHUNKS)
        def _():
            after_z(i)

        @pl.when(i == 1)
        def _():
            later_weights()

        @pl.when(jnp.logical_and(i >= 2, i < 2 + CHUNKS))
        def _():
            after_x(i - 2)

        @pl.when(i < CHUNKS)
        def _():
            local_part(i)

        @pl.when(i >= 4)
        def _():
            after_y(i - 4)
            finish(i - 4)

        return carry

    lax.fori_loop(0, 4 + CHUNKS, step, 0)

    for copies in (b_copies, c_copies):
        for copy in copies:
            copy.wait_send()
    tx_copy.wait_send()
    for d in (1, 2, 3):
        tz_copy(d).wait_send()
        ty_copy(d).wait_send()

    def drain(c, carry):
        for d in (1, 2, 3):
            z_copy(c, d).wait_send()

            @pl.when(y + d < 4)
            def _():
                y_copy(c, d).wait_send()

        x_copy(c).wait_send()
        return carry

    lax.fori_loop(0, CHUNKS, drain, 0)


def on_device(
    mixer_input, write_map, read_map, step_size, log_decay, skip_gain, level_table, level_index
):
    vmem, hbm = pl.BlockSpec(memory_space=pltpu.VMEM), pl.BlockSpec(memory_space=pl.ANY)
    dma = pltpu.SemaphoreType.DMA
    columns = HEADS * 64
    return pl.pallas_call(
        kernel,
        out_shape=pltpu.VMEM((TOKENS, columns), BF),
        in_specs=[hbm] * 6 + [vmem] * 3,
        out_specs=vmem,
        scratch_shapes=[
            pltpu.VMEM((CHUNKS, TOKENS, WIDE), BF),
            pltpu.VMEM((STATE, TOKENS), BF),
            pltpu.VMEM((STATE, TOKENS), BF),
            pltpu.VMEM((HEADS, TOKENS), F32),
            pltpu.VMEM((HEADS, TOKENS), F32),
            pltpu.VMEM((32, TOKENS), F32),
            pltpu.VMEM((32, TOKENS), F32),
            pltpu.VMEM((LEVELS, TOKENS), jnp.int32),
            pltpu.VMEM((16, TOKENS), F32),
            pltpu.VMEM((8, SUB), F32),
            pltpu.VMEM((SUB, SUB), F32),
            pltpu.VMEM((SUB, SUB), F32),
            pltpu.VMEM((CHUNKS, 8, TOKENS), F32),
            pltpu.VMEM((TOKENS, SUB), BF),
            pltpu.VMEM((TOKENS, 2 * SUB), BF),
            pltpu.VMEM((NSUB, SUB), F32),
            pltpu.VMEM((SUB, SUB), BF),
            pltpu.VMEM((CHUNKS, 64, WIDE), F32),
            pltpu.VMEM((4, CHUNKS, 2 * SUB, WIDE), BF),
            pltpu.VMEM((CHUNKS, SUB, 4 * SUB), BF),
            pltpu.VMEM((2 * SUB, LEVELS * SUB), BF),
            pltpu.VMEM((30, STATE, WIDE), F32),
            pltpu.VMEM((CHUNKS, len(LOCAL) * STATE, WIDE), BF),
            pltpu.VMEM((NSUB, SUB, SUB), F32),
            pltpu.VMEM((TOKENS, LEVELS * STATE), BF),
            pltpu.VMEM((TOKENS // 2, 4 * SUB), F32),
            pltpu.VMEM((TOKENS // 2, WIDE), F32),
            pltpu.VMEM((CHUNKS, TOKENS, WIDE), F32),
            pltpu.VMEM((CHUNKS, 4, STATE, WIDE), BF),
            pltpu.VMEM((CHUNKS, 2, STATE, WIDE), BF),
            pltpu.VMEM((CHUNKS, 4, STATE, WIDE), BF),
            pltpu.VMEM((CHUNKS, 5 * STATE, WIDE), BF),
            pltpu.VMEM((4, 8, SUB), F32),
            pltpu.VMEM((2, 8, SUB), F32),
            pltpu.VMEM((4, 8, SUB), F32),
            pltpu.VMEM((16, SUB), F32),
            pltpu.VMEM((CHUNKS, 16, WIDE), F32),
            pltpu.VMEM((CHUNKS, 16, WIDE), F32),
            dma((3,)), dma((3,)), dma((3,)), dma((3,)),
            dma((3,)), dma((3,)), dma(()), dma(()), dma((3,)), dma((3,)),
            dma((CHUNKS, 3)), dma((CHUNKS, 3)), dma((CHUNKS,)), dma((CHUNKS,)),
            dma((CHUNKS, 3)), dma((CHUNKS, 3)), dma((CHUNKS,)), dma((5,)),
        ],
        compiler_params=pltpu.CompilerParams(
            collective_id=0, has_side_effects=True, vmem_limit_bytes=54 * 2**20
        ),
    )(
        mixer_input,
        write_map.T,
        read_map.T,
        step_size,
        log_decay,
        level_index,
        skip_gain.reshape(1, HEADS),
        level_table.T,
        jnp.asarray(range_matrix(), BF),
    )


def solution(mesh):
    placed = (
        P("seq", "head"),
        P("seq", "head"),
        P("seq", "head"),
        P("head", "seq"),
        P("head", "seq"),
        P("head"),
        P(),
        P(None, "seq"),
    )
    return jax.shard_map(
        on_device, mesh=mesh, in_specs=placed, out_specs=P("seq", "head"), check_vma=False
    )
```
